128 devices in a mesh: chan: 16 (over x, y_hi, core), win: 8 (over y_lo, z).
Axes of the slice: x: 4, y: 4 (y_hi: 2, y_lo: 2; y = y_hi * 2 + y_lo), z: 4, core: 2. Of those that a mesh axis runs over, the one named last changes fastest.
Arguments:
- record: bfloat16 [3, 2048, 65536], P(None, 'chan', 'win'), may hold values from -6 to 6
- chan_taps: float32 [33], replicated, may hold values from -1 to 1
- time_taps: float32 [65], replicated, may hold values from -0.75 to 0.75
- sources: int32 [3, 4], replicated, may hold values from 0 to 2047
Outputs:
- stacked: float32 [3, 4, 129, 2048], P(None, None, None, 'chan')
The draws below stay inside these ranges and needn't reach their ends.
Inputs may be any that keep to these rules, and one draw needn't show every extreme that they name: `sources`: channel numbers of the fibre.
All inputs are finite; a program needn't handle non-finite values.
Results may differ from the reference program's by a relative error of at most 0.006.
Values may be sent and summed in bfloat16 or wider, within the bound.
A program may use at most 128 MiB of HBM per device.

```python
import math
import jax
import jax.numpy as jnp
from jax import lax

SAMP = 8192
STEPS = 3
SRC = 4
LAG = 64
CH_HALF = 16
TM_HALF = 32
CHANNELS = 2048
WINDOWS = 8


def with_ends(entries, stream_key, smallest, high):
    longest = entries.shape.index(max(entries.shape))
    spots = []
    for shift in (0, 1):
        where = [jax.random.randint(jax.random.fold_in(stream_key, axis), (), 0, length) for axis, length in enumerate(entries.shape)]
        where[longest] = (where[longest] + shift) % entries.shape[longest]
        spots.append(tuple(where))
    return entries.at[spots[0]].set(smallest).at[spots[1]].set(high)


def steps_of(rng, shape, split, low, top_value):
    loudness, own = 1.0, jax.random.fold_in(rng, 6)
    for position, parts in split:
        steps = jnp.exp(jax.random.uniform(jax.random.fold_in(own, position), (parts,), jnp.float32, low / len(split), top_value / len(split)))
        loudness = loudness * jnp.repeat(steps, shape[position] // parts).reshape([-1 if axis == position else 1 for axis in range(len(shape))])
    return loudness


def noise(stream_key, extent, width, reach, shards=(), kind=jnp.bfloat16):
    values = jax.random.normal(stream_key, extent, jnp.float32) * width
    if len(shards) > 0:
        values = steps_of(stream_key, extent, shards, -0.22, 0.18) * values
    return jnp.clip(values, min=-reach, max=reach).astype(kind)


def setup_inputs(seed: int = 0) -> dict:
    streams_of = jax.random.split(jax.random.key(seed), 5)
    return {
        "record": noise(streams_of[0], (STEPS, CHANNELS, WINDOWS * SAMP), 1.0, 6.0, ((1, 16), (2, 8))),
        "chan_taps": noise(streams_of[1], (2 * CH_HALF + 1,), (2 * CH_HALF + 1) ** -0.5, 1.0, (), jnp.float32),
        "time_taps": noise(streams_of[2], (2 * TM_HALF + 1,), (2 * TM_HALF + 1) ** -0.5, 0.75, (), jnp.float32),
        "sources": with_ends(jax.random.randint(streams_of[3], (STEPS, SRC), 0, CHANNELS), jax.random.fold_in(streams_of[3], 1), 0, CHANNELS - 1).astype(jnp.int32),
    }


def time_filter(chan_pass, tap_table):
    channels_here, samples = chan_pass.shape
    half = (tap_table.shape[0] - 1) // 2
    blocks = chan_pass.reshape(channels_here, samples // 128, 128)
    zeros_block = jnp.zeros_like(blocks[:, :1])
    earlier = jnp.concatenate([zeros_block, blocks[:, :-1]], axis=1)
    later = jnp.concatenate([blocks[:, 1:], zeros_block], axis=1)
    extended = jnp.concatenate([earlier, blocks, later], axis=2)
    offset = lax.iota(jnp.int32, 384)[:, None] - 128 - lax.iota(jnp.int32, 128)[None, :] + half
    inside = (offset >= 0) & (offset <= 2 * half)
    weights = jnp.where(inside, tap_table[jnp.clip(offset, 0, 2 * half)], jnp.zeros((), tap_table.dtype))
    result = jnp.einsum('cbr,rt->cbt', extended.astype(jnp.float32), weights.astype(jnp.float32))
    return result.reshape(channels_here, samples)

def whiten(time_pass):
    power = lax.optimization_barrier(jnp.mean(time_pass * time_pass, axis=-1, keepdims=True))
    return (time_pass * lax.rsqrt(power + 1e-06)).astype(jnp.bfloat16)

def correlate(whitened, panel):
    samples = whitened.shape[1]
    padded = jnp.pad(panel, ((0, 0), (LAG, LAG)))
    shifted = jnp.stack([padded[:, 2 * LAG - j:2 * LAG - j + samples] for j in range(2 * LAG + 1)], axis=-1)
    return jnp.einsum('cu,kuj->kjc', whitened.astype(jnp.float32), shifted.astype(jnp.float32))

def reference(record, chan_taps, time_taps, sources):
    chan_table = chan_taps.astype(jnp.bfloat16).astype(jnp.float32)
    time_table = time_taps.astype(jnp.bfloat16)
    half = (chan_taps.shape[0] - 1) // 2
    channels = record.shape[1]
    normalizer = 1.0 / math.sqrt(SAMP * WINDOWS)
    results = []
    for section in range(record.shape[0]):
        chosen = sources[section].astype(jnp.int32)

        def one_window(piece):
            padded = jnp.pad(piece.astype(jnp.float32), ((half, half), (0, 0)))
            total = jnp.zeros((channels, piece.shape[1]), jnp.float32)
            for k in range(2 * half + 1):
                total = total + chan_table[k] * padded[k:k + channels]
            chan_pass = total.astype(jnp.bfloat16)
            whitened = whiten(time_filter(chan_pass, time_table))
            panel = jnp.take(whitened, chosen, axis=0)
            return correlate(whitened, panel)
        pieces = record[section].reshape(channels, WINDOWS, SAMP).transpose(1, 0, 2)
        summed = lax.optimization_barrier(jnp.sum(lax.map(one_window, pieces), axis=0))
        results.append(summed * normalizer)
    return jnp.stack(results)
```

```python
import functools

import jax
import jax.numpy as jnp
from jax import lax
from jax.experimental import pallas as pl
from jax.experimental.pallas import tpu as pltpu
from jax.sharding import PartitionSpec as P

MESH = pl.DeviceIdType.MESH
bf = jnp.bfloat16
f32 = jnp.float32
STEPS, SRC, ROWS, SAMP = 3, 4, 128, 8192
CT, TT = 33, 65
EXT = SAMP + 256
QUART = SAMP // 4
HALO_CHUNKS = ((0, SAMP),), ((0, SAMP),), ((0, SAMP // 2), (SAMP // 2, SAMP))


def chan_peer(c, w, d):
    return (lax.rem(c + d + 16, 16), w)


def win_peer(c, w, d):
    return (c, lax.rem(w + d, 8))


def group_of(c):
    return (c // 4) * 2 + lax.rem(c, 2)


def group_peer(c, w, i):
    x, y, k = c // 4, lax.rem(c // 2, 2), lax.rem(c, 2)
    return (lax.rem(x + i // 2, 4) * 4 + y * 2 + lax.rem(k + i % 2, 2), w)


def side_peer(c, w):
    y = lax.rem(c // 2, 2)
    return ((c // 4) * 4 + (1 - y) * 2 + lax.rem(c, 2), w)


def remote(src, dst, send, recv, dev):
    return pltpu.make_async_remote_copy(
        src_ref=src, dst_ref=dst, send_sem=send, recv_sem=recv, device_id=dev, device_id_type=MESH
    )


def tap_row(taps, count, width):
    lane = lax.broadcasted_iota(jnp.int32, (8, 128), 1)
    row = jnp.zeros((8, 128), f32)
    for j in range(count):
        row = jnp.where(lane == j, taps[j], row)
    return jnp.concatenate([row[:1]] + [jnp.zeros((1, width - 128), f32)], axis=1)


def skewed(row, height, shift):
    base = jnp.broadcast_to(row, (height, row.shape[1]))
    return pltpu.roll(base, shift, 1, stride=1, stride_axis=0)


def time_blocks(cp, weights, b0, b1, group):
    height = cp.shape[0]
    for b in range(b0, b1, group):
        n = min(group, b1 - b)
        lhs = jnp.concatenate(
            [cp[:, 256 * (b + u) : 256 * (b + u) + 512] for u in range(n)], axis=0
        )
        r = jnp.dot(lhs, weights, preferred_element_type=f32)
        yield b, [r[u * height : (u + 1) * height] for u in range(n)]


def kernel(
    rec, ctaps, ttaps, src, out,
    xs, cpi, cpe, wt, pm, rr, acc, wm, part, pland, ysrc, yland, pbf, pag, pcp, pwn,
    rsrc, rland, red, agl,
    loc_sem, hs, hr, ps, pr, ys, yr, gs, gr, rs_s, rs_r, as_s, as_r,
):
    c = lax.axis_index("chan")
    w = lax.axis_index("win")
    g_me = group_of(c)
    loads = [
        pltpu.make_async_copy(rec.at[s], xs.at[s, pl.ds(16, ROWS)], loc_sem.at[s])
        for s in range(STEPS)
    ]
    for ld in loads:
        ld.start()
    bar = pltpu.get_barrier_semaphore()
    pl.semaphore_signal(bar, inc=1, device_id=chan_peer(c, w, 1), device_id_type=MESH)
    pl.semaphore_signal(bar, inc=1, device_id=chan_peer(c, w, -1), device_id_type=MESH)
    pl.semaphore_signal(bar, inc=1, device_id=side_peer(c, w), device_id_type=MESH)
    for i in range(1, 8):
        pl.semaphore_signal(bar, inc=1, device_id=group_peer(c, w, i), device_id_type=MESH)
        pl.semaphore_signal(bar, inc=1, device_id=win_peer(c, w, i), device_id_type=MESH)
    pl.semaphore_wait(bar, 17)

    halos = []
    n = 0
    for s in range(STEPS):
        for lo, hi in HALO_CHUNKS[s]:
            cols = pl.ds(lo, hi - lo)
            up = remote(
                rec.at[s, pl.ds(0, 16), cols], xs.at[s, pl.ds(144, 16), cols],
                hs.at[n], hr.at[n], chan_peer(c, w, -1),
            )
            down = remote(
                rec.at[s, pl.ds(112, 16), cols], xs.at[s, pl.ds(0, 16), cols],
                hs.at[n + 1], hr.at[n + 1], chan_peer(c, w, 1),
            )
            halos.append((up, down))
            n += 2
    for pair in halos:
        for cp in pair:
            cp.start()

    zpad = jnp.zeros((96, 128), bf)
    cpi[:, 0:128] = zpad
    cpi[:, SAMP + 128 : SAMP + 256] = zpad
    zpad = jnp.zeros((32, 128), bf)
    cpe[:, 0:128] = zpad
    cpe[:, SAMP + 128 : SAMP + 256] = zpad
    for s in range(STEPS):
        wt[s, ROWS : 2 * ROWS, SAMP : SAMP + 128] = jnp.zeros((ROWS, 128), bf)
        pwn[s, :, 0:128] = jnp.zeros((8, 128), f32)
        pwn[s, 4:8, 128 : SAMP + 128] = jnp.zeros((4, SAMP), f32)
        pwn[s, :, SAMP + 128 : SAMP + 256] = jnp.zeros((8, 128), f32)

    crow = tap_row(ctaps, CT, 256)
    b_in = skewed(crow, 96, 0)[:, :128].astype(bf)
    lane16 = lax.broadcasted_iota(jnp.int32, (16, 128), 1)
    top = skewed(crow, 16, 0)[:, :128]
    low = skewed(crow, 16, 48)[:, :128]
    top = jnp.where((lane16 < 16) & (c == 0), 0.0, top)
    low = jnp.where((lane16 >= 80) & (c == 15), 0.0, low)
    b_ed = jnp.concatenate([top, low], axis=0)[:, :96].astype(bf)
    wm[...] = jnp.transpose(skewed(tap_row(ttaps, TT, 512), 256, 96)).astype(bf)

    row16 = lax.broadcasted_iota(jnp.int32, (16, 128), 0)
    quarter = lax.broadcasted_iota(jnp.int32, (16, 256), 0) // 4
    for s in range(STEPS):
        want = jnp.zeros((16, 128), jnp.int32)
        for k in range(SRC):
            want = jnp.where(lax.rem(row16, 4) == k, src[s, k], want)
        off = lane16 - (want - c * ROWS) + 16
        pick = jnp.zeros((16, 128), f32)
        for j in range(CT):
            pick = jnp.where(off == j, ctaps[j], pick)
        pick = pick.astype(bf)
        loads[s].wait()
        got = jnp.dot(pick, xs[s, 16:144, :], preferred_element_type=f32)
        for g in range(8):
            val = got[:, 256 * g : 256 * g + 256]
            for q in range(1, 4):
                o = q * QUART + 256 * g
                val = jnp.where(quarter == q, got[:, o : o + 256], val)
            part[s, g] = val
        for i in range(1, 8):
            dev = group_peer(c, w, i)
            remote(
                part.at[s, group_of(dev[0])], pland.at[s, i],
                ps.at[8 * s + i], pr.at[8 * s + i], dev,
            ).start()

    def p_copy(s, i):
        dev = group_peer(c, w, i)
        return remote(
            part.at[s, group_of(dev[0])], pland.at[s, i], ps.at[8 * s + i], pr.at[8 * s + i], dev
        )

    def y_copy(s):
        return remote(ysrc.at[s], yland.at[s], ys.at[s], yr.at[s], side_peer(c, w))

    def g_copy(s, i):
        return remote(
            pbf.at[s], pag.at[s, g_me], gs.at[8 * s + i], gr.at[8 * s + i], group_peer(c, w, i)
        )

    def whiten_into(s, row, b, results, prev):
        cols = 256 * b
        y = jnp.concatenate(results, axis=1).astype(bf)
        width = y.shape[1]
        shifted = jnp.concatenate([prev, y[:, : width - 64]], axis=1)
        at = 0
        for r0, h in row:
            wt[s, ROWS + r0 : ROWS + r0 + h, cols : cols + width] = y[at : at + h]
            wt[s, r0 : r0 + h, cols : cols + width] = shifted[at : at + h]
            at += h
        return y[:, width - 64 :]

    def finish_w(s, row, prev):
        tail = jnp.concatenate([prev, jnp.zeros((prev.shape[0], 64), bf)], axis=1)
        at = 0
        for r0, h in row:
            wt[s, r0 : r0 + h, SAMP : SAMP + 128] = tail[at : at + h]
            at += h

    inner, edges = ((16, 96),), ((0, 16), (112, 16))

    def inner_pass(s):
        cpi[:, 128 : SAMP + 128] = jnp.dot(
            b_in, xs[s, 16:144, :], preferred_element_type=f32
        ).astype(bf)
        prev = jnp.zeros((96, 64), bf)
        total = jnp.zeros((96, 256), f32)
        for b, results in time_blocks(cpi, wm[...], 0, 32, 8):
            for r in results:
                total = total + r * r
            prev = whiten_into(s, inner, b, results, prev)
        finish_w(s, inner, prev)
        acc[s, 16:112, :] = total

    def edge_chan(s, lo, hi):
        both = jnp.concatenate([xs[s, 0:48, lo:hi], xs[s, 112:160, lo:hi]], axis=0)
        cpe[:, 128 + lo : 128 + hi] = jnp.dot(b_ed, both, preferred_element_type=f32).astype(bf)

    def edge_time(s, b0, b1, state):
        prev, total = state
        for b, results in time_blocks(cpe, wm[...], b0, b1, 16):
            for r in results:
                total = total + r * r
            prev = whiten_into(s, edges, b, results, prev)
        if b1 == 32:
            finish_w(s, edges, prev)
            acc[s, 0:16, :] = total[0:16]
            acc[s, 112:128, :] = total[16:32]
        return prev, total

    def edge_state():
        return jnp.zeros((32, 64), bf), jnp.zeros((32, 256), f32)

    def panel(s):
        x0 = pag[s, 0].astype(f32)[:, 0:128]
        x7 = pag[s, 7].astype(f32)[:, 128:256]
        z4 = jnp.zeros((4, 128), f32)
        pcp[:, 0:128] = jnp.concatenate([z4, x7[0:12]], axis=0).astype(bf)
        pcp[:, QUART + 128 : QUART + 256] = jnp.concatenate([x0[4:16], z4], axis=0).astype(bf)
        for g in range(8):
            pcp[:, 128 + 256 * g : 384 + 256 * g] = pag[s, g]
        (_, res), = time_blocks(pcp, wm[...], 0, 8, 8)
        tot = res[0] * res[0]
        for r in res[1:]:
            tot = tot + r * r
        tot = jnp.sum(tot, axis=1, keepdims=True)
        tot = tot[0:4] + tot[4:8] + tot[8:12] + tot[12:16]
        scale = lax.rsqrt(tot * (1.0 / SAMP) + 1e-6)
        scale = jnp.concatenate([scale] * 4, axis=0)
        full = jnp.concatenate([(r * scale).astype(bf).astype(f32) for r in res], axis=1)
        for q in range(4):
            pwn[s, 0:4, 128 + QUART * q : 128 + QUART * (q + 1)] = full[4 * q : 4 * q + 4]

    def build_p(s):
        for lo in range(0, SAMP + 128, 2048):
            n = min(2048, SAMP + 128 - lo)
            for k in range(SRC):
                row = pwn[s, k : k + 1, lo : lo + n + 128]
                pm[64 * k : 64 * k + 64, lo : lo + n] = skewed(row, 64, 0)[:, 128:].astype(bf)
            late = pwn[s, :, lo + 64 : lo + 64 + n]
            pm[256:272, lo : lo + n] = jnp.concatenate([late, late], axis=0).astype(bf)

    def corr(s, lo, hi, first):
        d = lax.dot_general(
            pm[:, lo:hi], wt[s, :, lo:hi], (((1,), (1,)), ((), ())), preferred_element_type=f32
        )
        rr[...] = d if first else rr[...] + d

    def r_copy(s, i):
        dev = win_peer(c, w, i)
        return remote(
            rsrc.at[s, dev[1]], rland.at[s, w], rs_s.at[8 * s + i], rs_r.at[8 * s + i], dev
        )

    def a_copy(s, i):
        return remote(
            red.at[s], agl.at[s, w], as_s.at[8 * s + i], as_r.at[8 * s + i], win_peer(c, w, i)
        )

    def send_corr(s):
        power = jnp.sum(jnp.transpose(acc[s]), axis=0, keepdims=True)
        scale = lax.rsqrt(power * (1.0 / SAMP) + 1e-6)
        scale = jnp.concatenate([scale, scale], axis=1)
        val = (rr[...] * scale).astype(bf)
        for k in range(8):
            rsrc[s, k, 0:32] = val[32 * k : 32 * k + 32]
            rsrc[s, k, 32:48] = val[256:272]
        for i in range(1, 8):
            r_copy(s, i).start()
        rland[s, w] = rsrc[s, w]

    norm = 1.0 / 256.0

    def reduce_corr(s):
        for i in range(1, 8):
            r_copy(s, i).wait()
        tot = rland[s, 0].astype(f32)
        for i in range(1, 8):
            tot = tot + rland[s, i].astype(f32)
        tot = tot * norm
        mine = tot[0:32].astype(bf)
        red[s] = mine
        for i in range(1, 8):
            a_copy(s, i).start()
        agl[s, w] = mine
        for k in range(SRC):
            out[s, k, 128:129, :] = tot[32 + k : 33 + k, 128:256]

    def write_out(s):
        for i in range(1, 8):
            a_copy(s, i).wait()
        for k in range(SRC):
            for h in range(2):
                val = agl[s, 2 * k + h].astype(f32)
                out[s, k, 32 * h : 32 * h + 32, :] = val[:, 0:128]
                out[s, k, 64 + 32 * h : 96 + 32 * h, :] = val[:, 128:256]

    def reduce_panel(s):
        for i in range(1, 8):
            p_copy(s, i).wait()
        tot = part[s, g_me]
        for i in range(1, 8):
            tot = tot + pland[s, i]
        ysrc[s] = tot
        y_copy(s).start()

    def share_panel(s):
        y_copy(s).wait()
        val = (ysrc[s] + yland[s]).astype(bf)
        pbf[s] = val
        for i in range(1, 8):
            g_copy(s, i).start()
        pag[s, g_me] = val

    def wait_panel(s):
        for i in range(1, 8):
            g_copy(s, i).wait()

    def wait_halo(j):
        for cp in halos[j]:
            cp.wait()

    inner_pass(0)
    for s in range(STEPS):
        reduce_panel(s)
    inner_pass(1)
    inner_pass(2)
    for s in range(STEPS):
        share_panel(s)
    wait_halo(0)
    edge_chan(0, 0, SAMP)
    edge_time(0, 0, 32, edge_state())
    wait_panel(0)
    panel(0)
    build_p(0)
    corr(0, 0, SAMP + 128, True)
    send_corr(0)
    wait_panel(1)
    panel(1)
    build_p(1)
    wait_halo(1)
    edge_chan(1, 0, SAMP)
    edge_time(1, 0, 32, edge_state())
    corr(1, 0, SAMP + 128, True)
    send_corr(1)
    reduce_corr(0)
    wait_panel(2)
    panel(2)
    build_p(2)
    wait_halo(2)
    edge_chan(2, 0, SAMP // 2)
    state = edge_time(2, 0, 15, edge_state())
    corr(2, 0, 3840, True)
    reduce_corr(1)
    wait_halo(3)
    edge_chan(2, SAMP // 2, SAMP)
    edge_time(2, 15, 32, state)
    corr(2, 3840, SAMP + 128, False)
    send_corr(2)
    write_out(0)
    write_out(1)
    reduce_corr(2)
    write_out(2)


def body(record, chan_taps, time_taps, sources):
    vm, dma = pltpu.VMEM, pltpu.SemaphoreType.DMA
    smem = pl.BlockSpec(memory_space=pltpu.SMEM)
    return pl.pallas_call(
        kernel,
        out_shape=jax.ShapeDtypeStruct((STEPS, SRC, 129, ROWS), f32),
        in_specs=[pl.BlockSpec(memory_space=pl.ANY), smem, smem, smem],
        out_specs=pl.BlockSpec(memory_space=pltpu.VMEM),
        scratch_shapes=[
            vm((STEPS, 160, SAMP), bf),
            vm((96, EXT), bf),
            vm((32, EXT), bf),
            vm((STEPS, 256, EXT), bf),
            vm((272, EXT), bf),
            vm((272, 256), f32),
            vm((STEPS, ROWS, 256), f32),
            vm((512, 256), bf),
            vm((STEPS, 8, 16, 256), f32),
            vm((STEPS, 8, 16, 256), f32),
            vm((STEPS, 16, 256), f32),
            vm((STEPS, 16, 256), f32),
            vm((STEPS, 16, 256), bf),
            vm((STEPS, 8, 16, 256), bf),
            vm((16, QUART + 256), bf),
            vm((STEPS, 8, EXT), f32),
            vm((STEPS, 8, 48, 256), bf),
            vm((STEPS, 8, 48, 256), bf),
            vm((STEPS, 32, 256), bf),
            vm((STEPS, 8, 32, 256), bf),
            dma((STEPS,)),
            dma((8,)), dma((8,)),
            dma((24,)), dma((24,)),
            dma((STEPS,)), dma((STEPS,)),
            dma((24,)), dma((24,)),
            dma((24,)), dma((24,)),
            dma((24,)), dma((24,)),
        ],
        compiler_params=pltpu.CompilerParams(
            collective_id=0, has_side_effects=True, vmem_limit_bytes=58 * 2**20
        ),
        name="xcorr",
    )(record, chan_taps, time_taps, sources)


def solution(mesh):
    in_specs = (P(None, "chan", "win"), P(), P(), P())
    out_specs = P(None, None, None, "chan")
    return jax.shard_map(body, mesh=mesh, in_specs=in_specs, out_specs=out_specs, check_vma=False)
```

```python
import functools

import jax
import jax.numpy as jnp
from jax import lax
from jax.experimental import pallas as pl
from jax.experimental.pallas import tpu as pltpu
from jax.sharding import PartitionSpec as P

MESH = pl.DeviceIdType.MESH
bf = jnp.bfloat16
f32 = jnp.float32
STEPS, SRC, ROWS, SAMP = 3, 4, 128, 8192
CT, TT = 33, 65
EXT = SAMP + 256
QUART = SAMP // 4
HALVES = ((0, SAMP // 2), (SAMP // 2, SAMP))
HALO_CHUNKS = (HALVES, HALVES, HALVES)
EARLY = 2
ORDER = (2, 0, 1)


def chan_peer(c, w, d):
    return (lax.rem(c + d + 16, 16), w)


def win_peer(c, w, d):
    return (c, lax.rem(w + d, 8))


def group_of(c):
    return (c // 4) * 2 + lax.rem(c, 2)


def group_peer(c, w, i):
    x, y, k = c // 4, lax.rem(c // 2, 2), lax.rem(c, 2)
    return (lax.rem(x + i // 2, 4) * 4 + y * 2 + lax.rem(k + i % 2, 2), w)


def side_peer(c, w):
    y = lax.rem(c // 2, 2)
    return ((c // 4) * 4 + (1 - y) * 2 + lax.rem(c, 2), w)


def remote(src, dst, send, recv, dev):
    return pltpu.make_async_remote_copy(
        src_ref=src, dst_ref=dst, send_sem=send, recv_sem=recv, device_id=dev, device_id_type=MESH
    )


def tap_row(taps, count, width):
    lane = lax.broadcasted_iota(jnp.int32, (8, 128), 1)
    row = jnp.zeros((8, 128), f32)
    for j in range(count):
        row = jnp.where(lane == j, taps[j], row)
    return jnp.concatenate([row[:1]] + [jnp.zeros((1, width - 128), f32)], axis=1)


def skewed(row, height, shift):
    base = jnp.broadcast_to(row, (height, row.shape[1]))
    return pltpu.roll(base, shift, 1, stride=1, stride_axis=0)


def time_blocks(cp, weights, b0, b1, group):
    height = cp.shape[0]
    for b in range(b0, b1, group):
        n = min(group, b1 - b)
        lhs = jnp.concatenate(
            [cp[:, 256 * (b + u) : 256 * (b + u) + 512] for u in range(n)], axis=0
        )
        r = jnp.dot(lhs, weights, preferred_element_type=f32)
        yield b, [r[u * height : (u + 1) * height] for u in range(n)]


def kernel(
    rec, ctaps, ttaps, src, out,
    xs, cpi, cpe, wt, pm, rr, acc, wm, part, pland, ysrc, yland, pbf, pag, pcp, pwn,
    zsrc, zland, vsrc, vland, red, agl, lates, wte, pm2, re, eacc, esrc, eland,
    loc_sem, hs, hr, ps, pr, ys, yr, gs, gr, zs, zr, vs, vr, as_, ar, es, er,
):
    c = lax.axis_index("chan")
    w = lax.axis_index("win")
    g_me = group_of(c)
    loads = [
        pltpu.make_async_copy(rec.at[s], xs.at[s, pl.ds(16, ROWS)], loc_sem.at[s])
        for s in range(STEPS)
    ]
    for s in ORDER:
        loads[s].start()
    bar = pltpu.get_barrier_semaphore()
    pl.semaphore_signal(bar, inc=1, device_id=chan_peer(c, w, 1), device_id_type=MESH)
    pl.semaphore_signal(bar, inc=1, device_id=chan_peer(c, w, -1), device_id_type=MESH)
    pl.semaphore_signal(bar, inc=1, device_id=side_peer(c, w), device_id_type=MESH)
    for i in range(1, 8):
        pl.semaphore_signal(bar, inc=1, device_id=group_peer(c, w, i), device_id_type=MESH)
        pl.semaphore_signal(bar, inc=1, device_id=win_peer(c, w, i), device_id_type=MESH)
    pl.semaphore_wait(bar, 17)

    halos = []
    n = 0
    for s in range(STEPS):
        for lo, hi in HALO_CHUNKS[s]:
            cols = pl.ds(lo, hi - lo)
            up = remote(
                rec.at[s, pl.ds(0, 16), cols], xs.at[s, pl.ds(144, 16), cols],
                hs.at[n], hr.at[n], chan_peer(c, w, -1),
            )
            down = remote(
                rec.at[s, pl.ds(112, 16), cols], xs.at[s, pl.ds(0, 16), cols],
                hs.at[n + 1], hr.at[n + 1], chan_peer(c, w, 1),
            )
            halos.append((up, down))
            n += 2
    for pair in halos[:EARLY]:
        for cp in pair:
            cp.start()

    row16 = lax.broadcasted_iota(jnp.int32, (16, 128), 0)
    quarter = lax.broadcasted_iota(jnp.int32, (16, 256), 0) // 4
    lane16 = lax.broadcasted_iota(jnp.int32, (16, 128), 1)
    for s in ORDER:
        want = jnp.zeros((16, 128), jnp.int32)
        for k in range(SRC):
            want = jnp.where(lax.rem(row16, 4) == k, src[s, k], want)
        off = lane16 - (want - c * ROWS) + 16
        pick = jnp.zeros((16, 128), f32)
        for j in range(CT):
            pick = jnp.where(off == j, ctaps[j], pick)
        pick = pick.astype(bf)
        loads[s].wait()
        got = jnp.dot(pick, xs[s, 16:144, :], preferred_element_type=f32)
        for g in range(8):
            val = got[:, 256 * g : 256 * g + 256]
            for q in range(1, 4):
                o = q * QUART + 256 * g
                val = jnp.where(quarter == q, got[:, o : o + 256], val)
            part[s, g] = val
        for i in range(1, 8):
            dev = group_peer(c, w, i)
            remote(
                part.at[s, group_of(dev[0])], pland.at[s, i],
                ps.at[8 * s + i], pr.at[8 * s + i], dev,
            ).start()

    zpad = jnp.zeros((96, 128), bf)
    cpi[:, 0:128] = zpad
    cpi[:, SAMP + 128 : SAMP + 256] = zpad
    zpad = jnp.zeros((32, 128), bf)
    cpe[:, 0:128] = zpad
    cpe[:, SAMP + 128 : SAMP + 256] = zpad
    for s in range(STEPS):
        wt[s, ROWS : 2 * ROWS, SAMP : SAMP + 128] = jnp.zeros((ROWS, 128), bf)
        pwn[s, :, 0:128] = jnp.zeros((8, 128), f32)
        pwn[s, 4:8, 128 : SAMP + 128] = jnp.zeros((4, SAMP), f32)
        pwn[s, :, SAMP + 128 : SAMP + 256] = jnp.zeros((8, 128), f32)

    for r0 in (0, 112, ROWS, ROWS + 112):
        wt[2, r0 : r0 + 16, 0 : SAMP + 128] = jnp.zeros((16, SAMP + 128), bf)
    wte[32:64, SAMP : SAMP + 128] = jnp.zeros((32, 128), bf)
    acc[2, 0:16, :] = jnp.zeros((16, 256), f32)
    acc[2, 112:128, :] = jnp.zeros((16, 256), f32)

    crow = tap_row(ctaps, CT, 256)
    b_in = skewed(crow, 96, 0)[:, :128].astype(bf)
    top = skewed(crow, 16, 0)[:, :128]
    low = skewed(crow, 16, 48)[:, :128]
    top = jnp.where((lane16 < 16) & (c == 0), 0.0, top)
    low = jnp.where((lane16 >= 80) & (c == 15), 0.0, low)
    b_ed = jnp.concatenate([top, low], axis=0)[:, :96].astype(bf)
    wm[...] = jnp.transpose(skewed(tap_row(ttaps, TT, 512), 256, 96)).astype(bf)

    def p_copy(s, i):
        dev = group_peer(c, w, i)
        return remote(
            part.at[s, group_of(dev[0])], pland.at[s, i], ps.at[8 * s + i], pr.at[8 * s + i], dev
        )

    def y_copy(s):
        return remote(ysrc.at[s], yland.at[s], ys.at[s], yr.at[s], side_peer(c, w))

    def g_copy(s, i):
        return remote(
            pbf.at[s], pag.at[s, g_me], gs.at[8 * s + i], gr.at[8 * s + i], group_peer(c, w, i)
        )

    def store_w(dst, half, rows, b, results, prev):
        cols = 256 * b
        y = jnp.concatenate(results, axis=1).astype(bf)
        width = y.shape[1]
        shifted = jnp.concatenate([prev, y[:, : width - 64]], axis=1)
        at = 0
        for r0, h in rows:
            dst[half + r0 : half + r0 + h, cols : cols + width] = y[at : at + h]
            dst[r0 : r0 + h, cols : cols + width] = shifted[at : at + h]
            at += h
        return y[:, width - 64 :]

    def finish_w(dst, rows, prev):
        tail = jnp.concatenate([prev, jnp.zeros((prev.shape[0], 64), bf)], axis=1)
        at = 0
        for r0, h in rows:
            dst[r0 : r0 + h, SAMP : SAMP + 128] = tail[at : at + h]
            at += h

    inner, edges, alone = ((16, 96),), ((0, 16), (112, 16)), ((0, 32),)

    def inner_pass(s):
        cpi[:, 128 : SAMP + 128] = jnp.dot(
            b_in, xs[s, 16:144, :], preferred_element_type=f32
        ).astype(bf)
        prev = jnp.zeros((96, 64), bf)
        total = jnp.zeros((96, 256), f32)
        for b, results in time_blocks(cpi, wm[...], 0, 32, 8):
            for r in results:
                total = total + r * r
            prev = store_w(wt.at[s], ROWS, inner, b, results, prev)
        finish_w(wt.at[s], inner, prev)
        acc[s, 16:112, :] = total

    def edge_chan(s, lo, hi):
        both = jnp.concatenate([xs[s, 0:48, lo:hi], xs[s, 112:160, lo:hi]], axis=0)
        cpe[:, 128 + lo : 128 + hi] = jnp.dot(b_ed, both, preferred_element_type=f32).astype(bf)

    def edge_time(s, b0, b1, state):
        prev, total = state
        dst, half, rows = (wte, 32, alone) if s == 2 else (wt.at[s], ROWS, edges)
        for b, results in time_blocks(cpe, wm[...], b0, b1, 16):
            for r in results:
                total = total + r * r
            prev = store_w(dst, half, rows, b, results, prev)
        if b1 == 32:
            finish_w(dst, rows, prev)
            if s == 2:
                eacc[...] = total
            else:
                acc[s, 0:16, :] = total[0:16]
                acc[s, 112:128, :] = total[16:32]
        return prev, total

    def edge_state():
        return jnp.zeros((32, 64), bf), jnp.zeros((32, 256), f32)

    def panel(s):
        x0 = pag[s, 0].astype(f32)[:, 0:128]
        x7 = pag[s, 7].astype(f32)[:, 128:256]
        z4 = jnp.zeros((4, 128), f32)
        pcp[:, 0:128] = jnp.concatenate([z4, x7[0:12]], axis=0).astype(bf)
        pcp[:, QUART + 128 : QUART + 256] = jnp.concatenate([x0[4:16], z4], axis=0).astype(bf)
        for g in range(8):
            pcp[:, 128 + 256 * g : 384 + 256 * g] = pag[s, g]
        (_, res), = time_blocks(pcp, wm[...], 0, 8, 8)
        tot = res[0] * res[0]
        for r in res[1:]:
            tot = tot + r * r
        tot = jnp.sum(tot, axis=1, keepdims=True)
        tot = tot[0:4] + tot[4:8] + tot[8:12] + tot[12:16]
        scale = lax.rsqrt(tot * (1.0 / SAMP) + 1e-6)
        scale = jnp.concatenate([scale] * 4, axis=0)
        full = jnp.concatenate([(r * scale).astype(bf).astype(f32) for r in res], axis=1)
        for q in range(4):
            pwn[s, 0:4, 128 + QUART * q : 128 + QUART * (q + 1)] = full[4 * q : 4 * q + 4]

    def build_piece(s, lo, hi):
        dst = pm2 if s == 2 else pm
        for k in range(SRC):
            row = pwn[s, k : k + 1, lo : hi + 128]
            dst[64 * k : 64 * k + 64, lo:hi] = skewed(row, 64, 0)[:, 128:].astype(bf)
        late = pwn[s, :, lo + 64 : hi + 64]
        dst[256:272, lo:hi] = jnp.concatenate([late, late], axis=0).astype(bf)

    def build_p(s):
        for lo in range(0, SAMP + 128, 2048):
            build_piece(s, lo, min(lo + 2048, SAMP + 128))

    def matmul_nt(lhs, rhs):
        return lax.dot_general(lhs, rhs, (((1,), (1,)), ((), ())), preferred_element_type=f32)

    def corr(s):
        hi = SAMP + 128
        rr[...] = matmul_nt((pm2 if s == 2 else pm)[:, 0:hi], wt[s, :, 0:hi])

    def edge_corr(lo, hi, first):
        d = matmul_nt(pm2[:, lo:hi], wte[:, lo:hi])
        re[...] = d if first else re[...] + d

    def scales(sums):
        power = jnp.sum(jnp.transpose(sums), axis=0, keepdims=True)
        scale = lax.rsqrt(power * (1.0 / SAMP) + 1e-6)
        return jnp.concatenate([scale, scale], axis=1)

    def z_peer(i):
        return (c, (w // 4) * 4 + lax.rem(w + i, 4))

    z_me = lax.rem(w, 4)

    def z_copy(s, i):
        dev = z_peer(i)
        return remote(
            zsrc.at[s, lax.rem(w + i, 4)], zland.at[s, i], zs.at[4 * s + i], zr.at[4 * s + i], dev
        )

    def v_copy(s):
        return remote(vsrc.at[s], vland.at[s], vs.at[s], vr.at[s], (c, lax.rem(w + 4, 8)))

    def a_copy(s, i):
        return remote(red.at[s], agl.at[s, z_me], as_.at[4 * s + i], ar.at[4 * s + i], z_peer(i))

    def e_copy(i):
        return remote(esrc, eland.at[w], es.at[i], er.at[i], win_peer(c, w, i))

    norm = 1.0 / 256.0

    def send_corr(s):
        val = rr[...] * scales(acc[s])
        lates[s] = val[256:264, 128:256]
        val = val.astype(bf)
        for k in range(SRC):
            zsrc[s, k, 0:64] = val[64 * k : 64 * k + 64]
        for i in range(1, 4):
            z_copy(s, i).start()

    def sum_z(s):
        for i in range(1, 4):
            z_copy(s, i).wait()
        tot = zsrc[s, z_me].astype(f32)
        for i in range(1, 4):
            tot = tot + zland[s, i].astype(f32)
        vsrc[s] = tot.astype(bf)
        v_copy(s).start()

    def sum_y(s):
        v_copy(s).wait()
        val = ((vsrc[s].astype(f32) + vland[s].astype(f32)) * norm).astype(bf)
        red[s] = val
        for i in range(1, 4):
            a_copy(s, i).start()
        agl[s, z_me] = val

    def wait_all(s):
        for i in range(1, 4):
            a_copy(s, i).wait()

    def write_out(s):
        wait_all(s)
        for k in range(SRC):
            out[s, k, 0:64, :] = agl[s, k, :, 0:128]
            out[s, k, 64:128, :] = agl[s, k, :, 128:256]

    def send_edges():
        val = re[...] * scales(eacc[...])
        fold = jnp.concatenate([val[0:128], val[128:256]], axis=1)
        late = jnp.concatenate([val[256:260], val[256:260]], axis=1)
        late = jnp.concatenate([late] + [lates[s][0:4] for s in range(STEPS)], axis=0)
        val = jnp.concatenate([fold, late], axis=0).astype(bf)
        esrc[...] = val
        for i in range(1, 8):
            e_copy(i).start()
        eland[w] = val

    def add_edges():
        for i in range(1, 8):
            e_copy(i).wait()
        tot = eland[0].astype(f32)
        for i in range(1, 8):
            tot = tot + eland[i].astype(f32)
        tot = tot * norm

        def spread(rows, at):
            mid = jnp.zeros((rows.shape[0], 96), f32)
            return jnp.concatenate([rows[:, at : at + 16], mid, rows[:, at + 16 : at + 32]], axis=1)

        blank = jnp.zeros((15, ROWS), f32)
        for k in range(SRC):
            rows = tot[64 * (k % 2) : 64 * (k % 2) + 64]
            at = 64 * (k // 2)
            for a in range(2):
                val = agl[2, k, :, 128 * a : 128 * a + 128].astype(f32) + spread(rows, at + 32 * a)
                out[2, k, 64 * a : 64 * a + 64, :] = val.astype(bf)
            for s in range(STEPS):
                val = tot[132 + 4 * s + k : 133 + 4 * s + k]
                if s == 2:
                    val = val + spread(tot[128 + k : 129 + k], 32)
                out[s, k, 128:144, :] = jnp.concatenate([val, blank], axis=0).astype(bf)

    def reduce_panel(s):
        for i in range(1, 8):
            p_copy(s, i).wait()
        tot = part[s, g_me]
        for i in range(1, 8):
            tot = tot + pland[s, i]
        ysrc[s] = tot
        y_copy(s).start()

    def share_panel(s):
        y_copy(s).wait()
        val = (ysrc[s] + yland[s]).astype(bf)
        pbf[s] = val
        for i in range(1, 8):
            g_copy(s, i).start()
        pag[s, g_me] = val

    def wait_panel(s):
        for i in range(1, 8):
            g_copy(s, i).wait()

    def wait_halo(j):
        for cp in halos[j]:
            cp.wait()

    inner_pass(2)
    for s in ORDER:
        reduce_panel(s)
    for pair in halos[EARLY:]:
        for cp in pair:
            cp.start()
    inner_pass(0)
    inner_pass(1)
    for s in ORDER:
        share_panel(s)
    wait_halo(0)
    wait_halo(1)
    edge_chan(0, 0, SAMP)
    edge_time(0, 0, 32, edge_state())
    wait_panel(2)
    panel(2)
    build_p(2)
    corr(2)
    send_corr(2)
    wait_panel(0)
    panel(0)
    build_p(0)
    corr(0)
    send_corr(0)
    wait_panel(1)
    panel(1)
    build_p(1)
    sum_z(2)
    wait_halo(2)
    wait_halo(3)
    edge_chan(1, 0, SAMP)
    edge_time(1, 0, 32, edge_state())
    corr(1)
    send_corr(1)
    sum_z(0)
    wait_halo(4)
    edge_chan(2, 0, SAMP // 2)
    state = edge_time(2, 0, 15, edge_state())
    edge_corr(0, 3840, True)
    sum_z(1)
    sum_y(2)
    wait_halo(5)
    edge_chan(2, SAMP // 2, SAMP)
    edge_time(2, 15, 32, state)
    edge_corr(3840, SAMP + 128, False)
    send_edges()
    sum_y(0)
    sum_y(1)
    write_out(0)
    write_out(1)
    wait_all(2)
    add_edges()


def body(record, chan_taps, time_taps, sources):
    vm, dma = pltpu.VMEM, pltpu.SemaphoreType.DMA
    smem = pl.BlockSpec(memory_space=pltpu.SMEM)
    packed = pl.pallas_call(
        kernel,
        out_shape=jax.ShapeDtypeStruct((STEPS, SRC, 144, ROWS), bf),
        in_specs=[pl.BlockSpec(memory_space=pl.ANY), smem, smem, smem],
        out_specs=pl.BlockSpec(memory_space=pltpu.VMEM),
        scratch_shapes=[
            vm((STEPS, 160, SAMP), bf),
            vm((96, EXT), bf),
            vm((32, EXT), bf),
            vm((STEPS, 256, EXT), bf),
            vm((272, EXT), bf),
            vm((272, 256), f32),
            vm((STEPS, ROWS, 256), f32),
            vm((512, 256), bf),
            vm((STEPS, 8, 16, 256), f32),
            vm((STEPS, 8, 16, 256), f32),
            vm((STEPS, 16, 256), f32),
            vm((STEPS, 16, 256), f32),
            vm((STEPS, 16, 256), bf),
            vm((STEPS, 8, 16, 256), bf),
            vm((16, QUART + 256), bf),
            vm((STEPS, 8, EXT), f32),
            vm((STEPS, 4, 64, 256), bf),
            vm((STEPS, 4, 64, 256), bf),
            vm((STEPS, 64, 256), bf),
            vm((STEPS, 64, 256), bf),
            vm((STEPS, 64, 256), bf),
            vm((STEPS, 4, 64, 256), bf),
            vm((STEPS, 8, 128), f32),
            vm((64, EXT), bf),
            vm((272, EXT), bf),
            vm((272, 64), f32),
            vm((32, 256), f32),
            vm((144, 128), bf),
            vm((8, 144, 128), bf),
            dma((STEPS,)),
            dma((12,)), dma((12,)),
            dma((24,)), dma((24,)),
            dma((STEPS,)), dma((STEPS,)),
            dma((24,)), dma((24,)),
            dma((12,)), dma((12,)),
            dma((STEPS,)), dma((STEPS,)),
            dma((12,)), dma((12,)),
            dma((8,)), dma((8,)),
        ],
        compiler_params=pltpu.CompilerParams(
            collective_id=0, has_side_effects=True, vmem_limit_bytes=58 * 2**20
        ),
        name="xcorr",
    )(record, chan_taps, time_taps, sources)
    return packed[:, :, :129].astype(f32)


def solution(mesh):
    in_specs = (P(None, "chan", "win"), P(), P(), P())
    out_specs = P(None, None, None, "chan")
    return jax.shard_map(body, mesh=mesh, in_specs=in_specs, out_specs=out_specs, check_vma=False)
```

```python
import functools

import jax
import jax.numpy as jnp
from jax import lax
from jax.experimental import pallas as pl
from jax.experimental.pallas import tpu as pltpu
from jax.sharding import PartitionSpec as P

MESH = pl.DeviceIdType.MESH
bf = jnp.bfloat16
f32 = jnp.float32
STEPS, SRC, ROWS, SAMP = 3, 4, 128, 8192
CT, TT = 33, 65
EXT = SAMP + 256
QUART = SAMP // 4
HALVES = ((0, SAMP // 2), (SAMP // 2, SAMP))
HALO_CHUNKS = (HALVES, HALVES, HALVES)
EARLY = 2
ORDER = (2, 0, 1)


def chan_peer(c, w, d):
    return (lax.rem(c + d + 16, 16), w)


def win_peer(c, w, d):
    return (c, lax.rem(w + d, 8))


def group_of(c):
    return (c // 4) * 2 + lax.rem(c, 2)


def group_peer(c, w, i):
    x, y, k = c // 4, lax.rem(c // 2, 2), lax.rem(c, 2)
    return (lax.rem(x + i // 2, 4) * 4 + y * 2 + lax.rem(k + i % 2, 2), w)


def side_peer(c, w):
    y = lax.rem(c // 2, 2)
    return ((c // 4) * 4 + (1 - y) * 2 + lax.rem(c, 2), w)


def remote(src, dst, send, recv, dev):
    return pltpu.make_async_remote_copy(
        src_ref=src, dst_ref=dst, send_sem=send, recv_sem=recv, device_id=dev, device_id_type=MESH
    )


def tap_row(taps, count, width):
    lane = lax.broadcasted_iota(jnp.int32, (8, 128), 1)
    row = jnp.zeros((8, 128), f32)
    for j in range(count):
        row = jnp.where(lane == j, taps[j], row)
    return jnp.concatenate([row[:1]] + [jnp.zeros((1, width - 128), f32)], axis=1)


def skewed(row, height, shift):
    base = jnp.broadcast_to(row, (height, row.shape[1]))
    return pltpu.roll(base, shift, 1, stride=1, stride_axis=0)


def time_blocks(cp, weights, b0, b1, group):
    height = cp.shape[0]
    for b in range(b0, b1, group):
        n = min(group, b1 - b)
        lhs = jnp.concatenate(
            [cp[:, 256 * (b + u) : 256 * (b + u) + 512] for u in range(n)], axis=0
        )
        r = jnp.dot(lhs, weights, preferred_element_type=f32)
        yield b, [r[u * height : (u + 1) * height] for u in range(n)]


def kernel(
    rec, ctaps_in, ttaps_in, src_in, out,
    ctaps, ttaps, src, small_sem,
    xs, cpi, cpe, wt, pm, rr, acc, wm, part, pland, ysrc, yland, pbf, pag, pcp, pwn,
    zsrc, zland, vsrc, vland, red, agl, lates, wte, pm2, re, eacc, esrc, eland,
    loc_sem, hs, hr, ps, pr, ys, yr, gs, gr, zs, zr, vs, vr, as_, ar, es, er,
):
    c = lax.axis_index("chan")
    w = lax.axis_index("win")
    g_me = group_of(c)
    loads = [
        pltpu.make_async_copy(rec.at[s], xs.at[s, pl.ds(16, ROWS)], loc_sem.at[s])
        for s in range(STEPS)
    ]
    for s in ORDER:
        loads[s].start()
    small = [
        pltpu.make_async_copy(a, b, small_sem.at[n])
        for n, (a, b) in enumerate(((ctaps_in, ctaps), (ttaps_in, ttaps), (src_in, src)))
    ]
    for cp in small:
        cp.start()
    bar = pltpu.get_barrier_semaphore()
    pl.semaphore_signal(bar, inc=1, device_id=chan_peer(c, w, 1), device_id_type=MESH)
    pl.semaphore_signal(bar, inc=1, device_id=chan_peer(c, w, -1), device_id_type=MESH)
    pl.semaphore_signal(bar, inc=1, device_id=side_peer(c, w), device_id_type=MESH)
    for i in range(1, 8):
        pl.semaphore_signal(bar, inc=1, device_id=group_peer(c, w, i), device_id_type=MESH)
        pl.semaphore_signal(bar, inc=1, device_id=win_peer(c, w, i), device_id_type=MESH)
    pl.semaphore_wait(bar, 17)

    halos = []
    n = 0
    for s in range(STEPS):
        for lo, hi in HALO_CHUNKS[s]:
            cols = pl.ds(lo, hi - lo)
            up = remote(
                rec.at[s, pl.ds(0, 16), cols], xs.at[s, pl.ds(144, 16), cols],
                hs.at[n], hr.at[n], chan_peer(c, w, -1),
            )
            down = remote(
                rec.at[s, pl.ds(112, 16), cols], xs.at[s, pl.ds(0, 16), cols],
                hs.at[n + 1], hr.at[n + 1], chan_peer(c, w, 1),
            )
            halos.append((up, down))
            n += 2
    for pair in halos[:EARLY]:
        for cp in pair:
            cp.start()

    for cp in small:
        cp.wait()
    row16 = lax.broadcasted_iota(jnp.int32, (16, 128), 0)
    quarter = lax.broadcasted_iota(jnp.int32, (16, 256), 0) // 4
    lane16 = lax.broadcasted_iota(jnp.int32, (16, 128), 1)
    for s in ORDER:
        want = jnp.zeros((16, 128), jnp.int32)
        for k in range(SRC):
            want = jnp.where(lax.rem(row16, 4) == k, src[s, k], want)
        off = lane16 - (want - c * ROWS) + 16
        pick = jnp.zeros((16, 128), f32)
        for j in range(CT):
            pick = jnp.where(off == j, ctaps[j], pick)
        pick = pick.astype(bf)
        loads[s].wait()
        got = jnp.dot(pick, xs[s, 16:144, :], preferred_element_type=f32)
        for g in range(8):
            val = got[:, 256 * g : 256 * g + 256]
            for q in range(1, 4):
                o = q * QUART + 256 * g
                val = jnp.where(quarter == q, got[:, o : o + 256], val)
            part[s, g] = val
        for i in range(1, 8):
            dev = group_peer(c, w, i)
            remote(
                part.at[s, group_of(dev[0])], pland.at[s, i],
                ps.at[8 * s + i], pr.at[8 * s + i], dev,
            ).start()

    zpad = jnp.zeros((96, 128), bf)
    cpi[:, 0:128] = zpad
    cpi[:, SAMP + 128 : SAMP + 256] = zpad
    zpad = jnp.zeros((32, 128), bf)
    cpe[:, 0:128] = zpad
    cpe[:, SAMP + 128 : SAMP + 256] = zpad
    for s in range(STEPS):
        wt[s, ROWS : 2 * ROWS, SAMP : SAMP + 128] = jnp.zeros((ROWS, 128), bf)
        pwn[s, :, 0:128] = jnp.zeros((8, 128), f32)
        pwn[s, 4:8, 128 : SAMP + 128] = jnp.zeros((4, SAMP), f32)
        pwn[s, :, SAMP + 128 : SAMP + 256] = jnp.zeros((8, 128), f32)

    for r0 in (0, 112, ROWS, ROWS + 112):
        wt[2, r0 : r0 + 16, 0 : SAMP + 128] = jnp.zeros((16, SAMP + 128), bf)
    wte[32:64, SAMP : SAMP + 128] = jnp.zeros((32, 128), bf)
    acc[2, 0:16, :] = jnp.zeros((16, 256), f32)
    acc[2, 112:128, :] = jnp.zeros((16, 256), f32)

    crow = tap_row(ctaps, CT, 256)
    b_in = skewed(crow, 96, 0)[:, :128].astype(bf)
    top = skewed(crow, 16, 0)[:, :128]
    low = skewed(crow, 16, 48)[:, :128]
    top = jnp.where((lane16 < 16) & (c == 0), 0.0, top)
    low = jnp.where((lane16 >= 80) & (c == 15), 0.0, low)
    b_ed = jnp.concatenate([top, low], axis=0)[:, :96].astype(bf)
    wm[...] = jnp.transpose(skewed(tap_row(ttaps, TT, 512), 256, 96)).astype(bf)

    def p_copy(s, i):
        dev = group_peer(c, w, i)
        return remote(
            part.at[s, group_of(dev[0])], pland.at[s, i], ps.at[8 * s + i], pr.at[8 * s + i], dev
        )

    def y_copy(s):
        return remote(ysrc.at[s], yland.at[s], ys.at[s], yr.at[s], side_peer(c, w))

    def g_copy(s, i):
        return remote(
            pbf.at[s], pag.at[s, g_me], gs.at[8 * s + i], gr.at[8 * s + i], group_peer(c, w, i)
        )

    def store_w(dst, half, rows, b, results, prev):
        cols = 256 * b
        y = jnp.concatenate(results, axis=1).astype(bf)
        width = y.shape[1]
        shifted = jnp.concatenate([prev, y[:, : width - 64]], axis=1)
        at = 0
        for r0, h in rows:
            dst[half + r0 : half + r0 + h, cols : cols + width] = y[at : at + h]
            dst[r0 : r0 + h, cols : cols + width] = shifted[at : at + h]
            at += h
        return y[:, width - 64 :]

    def finish_w(dst, rows, prev):
        tail = jnp.concatenate([prev, jnp.zeros((prev.shape[0], 64), bf)], axis=1)
        at = 0
        for r0, h in rows:
            dst[r0 : r0 + h, SAMP : SAMP + 128] = tail[at : at + h]
            at += h

    inner, edges, alone = ((16, 96),), ((0, 16), (112, 16)), ((0, 32),)

    def inner_pass(s):
        cpi[:, 128 : SAMP + 128] = jnp.dot(
            b_in, xs[s, 16:144, :], preferred_element_type=f32
        ).astype(bf)
        prev = jnp.zeros((96, 64), bf)
        total = jnp.zeros((96, 256), f32)
        for b, results in time_blocks(cpi, wm[...], 0, 32, 8):
            for r in results:
                total = total + r * r
            prev = store_w(wt.at[s], ROWS, inner, b, results, prev)
        finish_w(wt.at[s], inner, prev)
        acc[s, 16:112, :] = total

    def edge_chan(s, lo, hi):
        both = jnp.concatenate([xs[s, 0:48, lo:hi], xs[s, 112:160, lo:hi]], axis=0)
        cpe[:, 128 + lo : 128 + hi] = jnp.dot(b_ed, both, preferred_element_type=f32).astype(bf)

    def edge_time(s, b0, b1, state):
        prev, total = state
        dst, half, rows = (wte, 32, alone) if s == 2 else (wt.at[s], ROWS, edges)
        for b, results in time_blocks(cpe, wm[...], b0, b1, 16):
            for r in results:
                total = total + r * r
            prev = store_w(dst, half, rows, b, results, prev)
        if b1 == 32:
            finish_w(dst, rows, prev)
            if s == 2:
                eacc[...] = total
            else:
                acc[s, 0:16, :] = total[0:16]
                acc[s, 112:128, :] = total[16:32]
        return prev, total

    def edge_state():
        return jnp.zeros((32, 64), bf), jnp.zeros((32, 256), f32)

    def panel(s):
        x0 = pag[s, 0].astype(f32)[:, 0:128]
        x7 = pag[s, 7].astype(f32)[:, 128:256]
        z4 = jnp.zeros((4, 128), f32)
        pcp[:, 0:128] = jnp.concatenate([z4, x7[0:12]], axis=0).astype(bf)
        pcp[:, QUART + 128 : QUART + 256] = jnp.concatenate([x0[4:16], z4], axis=0).astype(bf)
        for g in range(8):
            pcp[:, 128 + 256 * g : 384 + 256 * g] = pag[s, g]
        (_, res), = time_blocks(pcp, wm[...], 0, 8, 8)
        tot = res[0] * res[0]
        for r in res[1:]:
            tot = tot + r * r
        tot = jnp.sum(tot, axis=1, keepdims=True)
        tot = tot[0:4] + tot[4:8] + tot[8:12] + tot[12:16]
        scale = lax.rsqrt(tot * (1.0 / SAMP) + 1e-6)
        scale = jnp.concatenate([scale] * 4, axis=0)
        full = jnp.concatenate([(r * scale).astype(bf).astype(f32) for r in res], axis=1)
        for q in range(4):
            pwn[s, 0:4, 128 + QUART * q : 128 + QUART * (q + 1)] = full[4 * q : 4 * q + 4]

    def build_piece(s, lo, hi):
        dst = pm2 if s == 2 else pm
        for k in range(SRC):
            row = pwn[s, k : k + 1, lo : hi + 128]
            dst[64 * k : 64 * k + 64, lo:hi] = skewed(row, 64, 0)[:, 128:].astype(bf)
        late = pwn[s, :, lo + 64 : hi + 64]
        dst[256:272, lo:hi] = jnp.concatenate([late, late], axis=0).astype(bf)

    def build_p(s):
        for lo in range(0, SAMP + 128, 2048):
            build_piece(s, lo, min(lo + 2048, SAMP + 128))

    def matmul_nt(lhs, rhs):
        return lax.dot_general(lhs, rhs, (((1,), (1,)), ((), ())), preferred_element_type=f32)

    def corr(s):
        hi = SAMP + 128
        rr[...] = matmul_nt((pm2 if s == 2 else pm)[:, 0:hi], wt[s, :, 0:hi])

    def edge_corr(lo, hi, first):
        d = matmul_nt(pm2[:, lo:hi], wte[:, lo:hi])
        re[...] = d if first else re[...] + d

    def scales(sums):
        power = jnp.sum(jnp.transpose(sums), axis=0, keepdims=True)
        scale = lax.rsqrt(power * (1.0 / SAMP) + 1e-6)
        return jnp.concatenate([scale, scale], axis=1)

    def z_peer(i):
        return (c, (w // 4) * 4 + lax.rem(w + i, 4))

    z_me = lax.rem(w, 4)

    def z_copy(s, i):
        dev = z_peer(i)
        return remote(
            zsrc.at[s, lax.rem(w + i, 4)], zland.at[s, i], zs.at[4 * s + i], zr.at[4 * s + i], dev
        )

    def v_copy(s):
        return remote(vsrc.at[s], vland.at[s], vs.at[s], vr.at[s], (c, lax.rem(w + 4, 8)))

    def a_copy(s, i):
        return remote(red.at[s], agl.at[s, z_me], as_.at[4 * s + i], ar.at[4 * s + i], z_peer(i))

    def e_copy(i):
        return remote(esrc, eland.at[w], es.at[i], er.at[i], win_peer(c, w, i))

    norm = 1.0 / 256.0

    def send_corr(s):
        val = rr[...] * scales(acc[s])
        lates[s] = val[256:264, 128:256]
        val = val.astype(bf)
        for k in range(SRC):
            zsrc[s, k, 0:64] = val[64 * k : 64 * k + 64]
        for i in range(1, 4):
            z_copy(s, i).start()

    def sum_z(s):
        for i in range(1, 4):
            z_copy(s, i).wait()
        tot = zsrc[s, z_me].astype(f32)
        for i in range(1, 4):
            tot = tot + zland[s, i].astype(f32)
        vsrc[s] = tot.astype(bf)
        v_copy(s).start()

    def sum_y(s):
        v_copy(s).wait()
        val = ((vsrc[s].astype(f32) + vland[s].astype(f32)) * norm).astype(bf)
        red[s] = val
        for i in range(1, 4):
            a_copy(s, i).start()
        agl[s, z_me] = val

    def wait_all(s):
        for i in range(1, 4):
            a_copy(s, i).wait()

    def write_out(s):
        wait_all(s)
        for k in range(SRC):
            out[s, k, 0:64, :] = agl[s, k, :, 0:128]
            out[s, k, 64:128, :] = agl[s, k, :, 128:256]

    def send_edges():
        val = re[...] * scales(eacc[...])
        fold = jnp.concatenate([val[0:128], val[128:256]], axis=1)
        late = jnp.concatenate([val[256:260], val[256:260]], axis=1)
        late = jnp.concatenate([late] + [lates[s][0:4] for s in range(STEPS)], axis=0)
        val = jnp.concatenate([fold, late], axis=0).astype(bf)
        esrc[...] = val
        for i in range(1, 8):
            e_copy(i).start()
        eland[w] = val

    def add_edges():
        for i in range(1, 8):
            e_copy(i).wait()
        tot = eland[0].astype(f32)
        for i in range(1, 8):
            tot = tot + eland[i].astype(f32)
        tot = tot * norm

        def spread(rows, at):
            mid = jnp.zeros((rows.shape[0], 96), f32)
            return jnp.concatenate([rows[:, at : at + 16], mid, rows[:, at + 16 : at + 32]], axis=1)

        blank = jnp.zeros((15, ROWS), f32)
        for k in range(SRC):
            rows = tot[64 * (k % 2) : 64 * (k % 2) + 64]
            at = 64 * (k // 2)
            for a in range(2):
                val = agl[2, k, :, 128 * a : 128 * a + 128].astype(f32) + spread(rows, at + 32 * a)
                out[2, k, 64 * a : 64 * a + 64, :] = val.astype(bf)
            for s in range(STEPS):
                val = tot[132 + 4 * s + k : 133 + 4 * s + k]
                if s == 2:
                    val = val + spread(tot[128 + k : 129 + k], 32)
                out[s, k, 128:144, :] = jnp.concatenate([val, blank], axis=0).astype(bf)

    def reduce_panel(s):
        for i in range(1, 8):
            p_copy(s, i).wait()
        tot = part[s, g_me]
        for i in range(1, 8):
            tot = tot + pland[s, i]
        ysrc[s] = tot
        y_copy(s).start()

    def share_panel(s):
        y_copy(s).wait()
        val = (ysrc[s] + yland[s]).astype(bf)
        pbf[s] = val
        for i in range(1, 8):
            g_copy(s, i).start()
        pag[s, g_me] = val

    def wait_panel(s):
        for i in range(1, 8):
            g_copy(s, i).wait()

    def wait_halo(j):
        for cp in halos[j]:
            cp.wait()

    inner_pass(2)
    for s in ORDER:
        reduce_panel(s)
    for pair in halos[EARLY:]:
        for cp in pair:
            cp.start()
    inner_pass(0)
    inner_pass(1)
    for s in ORDER:
        share_panel(s)
    wait_halo(0)
    wait_halo(1)
    edge_chan(0, 0, SAMP)
    edge_time(0, 0, 32, edge_state())
    wait_panel(2)
    panel(2)
    build_p(2)
    corr(2)
    send_corr(2)
    wait_panel(0)
    panel(0)
    build_p(0)
    corr(0)
    send_corr(0)
    wait_panel(1)
    panel(1)
    build_p(1)
    sum_z(2)
    wait_halo(2)
    wait_halo(3)
    edge_chan(1, 0, SAMP)
    edge_time(1, 0, 32, edge_state())
    corr(1)
    send_corr(1)
    sum_z(0)
    wait_halo(4)
    edge_chan(2, 0, SAMP // 2)
    state = edge_time(2, 0, 15, edge_state())
    edge_corr(0, 3840, True)
    sum_z(1)
    sum_y(2)
    wait_halo(5)
    edge_chan(2, SAMP // 2, SAMP)
    edge_time(2, 15, 32, state)
    edge_corr(3840, SAMP + 128, False)
    send_edges()
    sum_y(0)
    sum_y(1)
    write_out(0)
    write_out(1)
    wait_all(2)
    add_edges()


def body(record, chan_taps, time_taps, sources):
    vm, dma = pltpu.VMEM, pltpu.SemaphoreType.DMA
    sm = pltpu.SMEM
    packed = pl.pallas_call(
        kernel,
        out_shape=jax.ShapeDtypeStruct((STEPS, SRC, 144, ROWS), bf),
        in_specs=[pl.BlockSpec(memory_space=pl.ANY)] * 4,
        out_specs=pl.BlockSpec(memory_space=pltpu.VMEM),
        scratch_shapes=[
            sm((CT,), f32),
            sm((TT,), f32),
            sm((STEPS, SRC), jnp.int32),
            dma((3,)),
            vm((STEPS, 160, SAMP), bf),
            vm((96, EXT), bf),
            vm((32, EXT), bf),
            vm((STEPS, 256, EXT), bf),
            vm((272, EXT), bf),
            vm((272, 256), f32),
            vm((STEPS, ROWS, 256), f32),
            vm((512, 256), bf),
            vm((STEPS, 8, 16, 256), f32),
            vm((STEPS, 8, 16, 256), f32),
            vm((STEPS, 16, 256), f32),
            vm((STEPS, 16, 256), f32),
            vm((STEPS, 16, 256), bf),
            vm((STEPS, 8, 16, 256), bf),
            vm((16, QUART + 256), bf),
            vm((STEPS, 8, EXT), f32),
            vm((STEPS, 4, 64, 256), bf),
            vm((STEPS, 4, 64, 256), bf),
            vm((STEPS, 64, 256), bf),
            vm((STEPS, 64, 256), bf),
            vm((STEPS, 64, 256), bf),
            vm((STEPS, 4, 64, 256), bf),
            vm((STEPS, 8, 128), f32),
            vm((64, EXT), bf),
            vm((272, EXT), bf),
            vm((272, 64), f32),
            vm((32, 256), f32),
            vm((144, 128), bf),
            vm((8, 144, 128), bf),
            dma((STEPS,)),
            dma((12,)), dma((12,)),
            dma((24,)), dma((24,)),
            dma((STEPS,)), dma((STEPS,)),
            dma((24,)), dma((24,)),
            dma((12,)), dma((12,)),
            dma((STEPS,)), dma((STEPS,)),
            dma((12,)), dma((12,)),
            dma((8,)), dma((8,)),
        ],
        compiler_params=pltpu.CompilerParams(
            collective_id=0, has_side_effects=True, vmem_limit_bytes=58 * 2**20
        ),
        name="xcorr",
    )(record, chan_taps, time_taps, sources)
    return packed[:, :, :129].astype(f32)


def solution(mesh):
    in_specs = (P(None, "chan", "win"), P(), P(), P())
    out_specs = P(None, None, None, "chan")
    return jax.shard_map(body, mesh=mesh, in_specs=in_specs, out_specs=out_specs, check_vma=False)
```

```python
import functools

import jax
import jax.numpy as jnp
from jax import lax
from jax.experimental import pallas as pl
from jax.experimental.pallas import tpu as pltpu
from jax.sharding import PartitionSpec as P

MESH = pl.DeviceIdType.MESH
bf = jnp.bfloat16
f32 = jnp.float32
STEPS, SRC, ROWS, SAMP = 3, 4, 128, 8192
CT, TT = 33, 65
EXT = SAMP + 256
QUART = SAMP // 4
HALVES = ((0, SAMP // 2), (SAMP // 2, SAMP))
HALO_CHUNKS = (HALVES, HALVES, HALVES)
EARLY = 3
ORDER = (2, 0, 1)


def chan_peer(c, w, d):
    return (lax.rem(c + d + 16, 16), w)


def win_peer(c, w, d):
    return (c, lax.rem(w + d, 8))


def group_of(c):
    return (c // 4) * 2 + lax.rem(c, 2)


def group_peer(c, w, i):
    x, y, k = c // 4, lax.rem(c // 2, 2), lax.rem(c, 2)
    return (lax.rem(x + i // 2, 4) * 4 + y * 2 + lax.rem(k + i % 2, 2), w)


def side_peer(c, w):
    y = lax.rem(c // 2, 2)
    return ((c // 4) * 4 + (1 - y) * 2 + lax.rem(c, 2), w)


def remote(src, dst, send, recv, dev):
    return pltpu.make_async_remote_copy(
        src_ref=src, dst_ref=dst, send_sem=send, recv_sem=recv, device_id=dev, device_id_type=MESH
    )


def tap_row(taps, count, width):
    lane = lax.broadcasted_iota(jnp.int32, (8, 128), 1)
    row = jnp.zeros((8, 128), f32)
    for j in range(count):
        row = jnp.where(lane == j, taps[j], row)
    return jnp.concatenate([row[:1]] + [jnp.zeros((1, width - 128), f32)], axis=1)


def skewed(row, height, shift):
    base = jnp.broadcast_to(row, (height, row.shape[1]))
    return pltpu.roll(base, shift, 1, stride=1, stride_axis=0)


def time_blocks(cp, weights, b0, b1, group):
    height = cp.shape[0]
    for b in range(b0, b1, group):
        n = min(group, b1 - b)
        lhs = jnp.concatenate(
            [cp[:, 256 * (b + u) : 256 * (b + u) + 512] for u in range(n)], axis=0
        )
        r = jnp.dot(lhs, weights, preferred_element_type=f32)
        yield b, [r[u * height : (u + 1) * height] for u in range(n)]


def kernel(
    rec, ctaps_in, ttaps_in, src_in, out,
    ctaps, ttaps, src, small_sem,
    xs, cpi, cpe, wt, pm, rr, acc, wm, part, pland, ysrc, yland, pbf, pag, pcp, pwn,
    zsrc, zland, vsrc, vland, red, agl, lates, wte, pm2, re, eacc, esrc, eland,
    loc_sem, hs, hr, ps, pr, ys, yr, gs, gr, zs, zr, vs, vr, as_, ar, es, er,
):
    c = lax.axis_index("chan")
    w = lax.axis_index("win")
    g_me = group_of(c)
    loads = [
        pltpu.make_async_copy(rec.at[s], xs.at[s, pl.ds(16, ROWS)], loc_sem.at[s])
        for s in range(STEPS)
    ]
    for s in ORDER:
        loads[s].start()
    small = [
        pltpu.make_async_copy(a, b, small_sem.at[n])
        for n, (a, b) in enumerate(((ctaps_in, ctaps), (ttaps_in, ttaps), (src_in, src)))
    ]
    for cp in small:
        cp.start()
    bar = pltpu.get_barrier_semaphore()
    pl.semaphore_signal(bar, inc=1, device_id=chan_peer(c, w, 1), device_id_type=MESH)
    pl.semaphore_signal(bar, inc=1, device_id=chan_peer(c, w, -1), device_id_type=MESH)
    pl.semaphore_signal(bar, inc=1, device_id=side_peer(c, w), device_id_type=MESH)
    for i in range(1, 8):
        pl.semaphore_signal(bar, inc=1, device_id=group_peer(c, w, i), device_id_type=MESH)
        pl.semaphore_signal(bar, inc=1, device_id=win_peer(c, w, i), device_id_type=MESH)
    pl.semaphore_wait(bar, 17)

    halos = []
    n = 0
    for s in range(STEPS):
        for lo, hi in HALO_CHUNKS[s]:
            cols = pl.ds(lo, hi - lo)
            up = remote(
                rec.at[s, pl.ds(0, 16), cols], xs.at[s, pl.ds(144, 16), cols],
                hs.at[n], hr.at[n], chan_peer(c, w, -1),
            )
            down = remote(
                rec.at[s, pl.ds(112, 16), cols], xs.at[s, pl.ds(0, 16), cols],
                hs.at[n + 1], hr.at[n + 1], chan_peer(c, w, 1),
            )
            halos.append((up, down))
            n += 2
    for pair in halos[:EARLY]:
        for cp in pair:
            cp.start()

    for cp in small:
        cp.wait()
    row16 = lax.broadcasted_iota(jnp.int32, (16, 128), 0)
    quarter = lax.broadcasted_iota(jnp.int32, (16, 256), 0) // 4
    lane16 = lax.broadcasted_iota(jnp.int32, (16, 128), 1)
    for s in ORDER:
        want = jnp.zeros((16, 128), jnp.int32)
        for k in range(SRC):
            want = jnp.where(lax.rem(row16, 4) == k, src[s, k], want)
        off = lane16 - (want - c * ROWS) + 16
        pick = jnp.zeros((16, 128), f32)
        for j in range(CT):
            pick = jnp.where(off == j, ctaps[j], pick)
        pick = pick.astype(bf)
        loads[s].wait()
        got = jnp.dot(pick, xs[s, 16:144, :], preferred_element_type=f32)
        for g in range(8):
            val = got[:, 256 * g : 256 * g + 256]
            for q in range(1, 4):
                o = q * QUART + 256 * g
                val = jnp.where(quarter == q, got[:, o : o + 256], val)
            part[s, g] = val
        for i in range(1, 8):
            dev = group_peer(c, w, i)
            remote(
                part.at[s, group_of(dev[0])], pland.at[s, i],
                ps.at[8 * s + i], pr.at[8 * s + i], dev,
            ).start()

    zpad = jnp.zeros((96, 128), bf)
    cpi[:, 0:128] = zpad
    cpi[:, SAMP + 128 : SAMP + 256] = zpad
    zpad = jnp.zeros((32, 128), bf)
    cpe[:, 0:128] = zpad
    cpe[:, SAMP + 128 : SAMP + 256] = zpad
    for s in range(STEPS):
        wt[s, ROWS : 2 * ROWS, SAMP : SAMP + 128] = jnp.zeros((ROWS, 128), bf)
        pwn[s, :, 0:128] = jnp.zeros((8, 128), f32)
        pwn[s, 4:8, 128 : SAMP + 128] = jnp.zeros((4, SAMP), f32)
        pwn[s, :, SAMP + 128 : SAMP + 256] = jnp.zeros((8, 128), f32)

    for r0 in (0, 112, ROWS, ROWS + 112):
        wt[2, r0 : r0 + 16, 0 : SAMP + 128] = jnp.zeros((16, SAMP + 128), bf)
    wte[32:64, SAMP : SAMP + 128] = jnp.zeros((32, 128), bf)
    acc[2, 0:16, :] = jnp.zeros((16, 256), f32)
    acc[2, 112:128, :] = jnp.zeros((16, 256), f32)

    crow = tap_row(ctaps, CT, 256)
    b_in = skewed(crow, 96, 0)[:, :128].astype(bf)
    top = skewed(crow, 16, 0)[:, :128]
    low = skewed(crow, 16, 48)[:, :128]
    top = jnp.where((lane16 < 16) & (c == 0), 0.0, top)
    low = jnp.where((lane16 >= 80) & (c == 15), 0.0, low)
    b_ed = jnp.concatenate([top, low], axis=0)[:, :96].astype(bf)
    wm[...] = jnp.transpose(skewed(tap_row(ttaps, TT, 512), 256, 96)).astype(bf)

    def p_copy(s, i):
        dev = group_peer(c, w, i)
        return remote(
            part.at[s, group_of(dev[0])], pland.at[s, i], ps.at[8 * s + i], pr.at[8 * s + i], dev
        )

    def y_copy(s):
        return remote(ysrc.at[s], yland.at[s], ys.at[s], yr.at[s], side_peer(c, w))

    def g_copy(s, i):
        return remote(
            pbf.at[s], pag.at[s, g_me], gs.at[8 * s + i], gr.at[8 * s + i], group_peer(c, w, i)
        )

    def store_w(dst, half, rows, b, results, prev):
        cols = 256 * b
        y = jnp.concatenate(results, axis=1).astype(bf)
        width = y.shape[1]
        shifted = jnp.concatenate([prev, y[:, : width - 64]], axis=1)
        at = 0
        for r0, h in rows:
            dst[half + r0 : half + r0 + h, cols : cols + width] = y[at : at + h]
            dst[r0 : r0 + h, cols : cols + width] = shifted[at : at + h]
            at += h
        return y[:, width - 64 :]

    def finish_w(dst, rows, prev):
        tail = jnp.concatenate([prev, jnp.zeros((prev.shape[0], 64), bf)], axis=1)
        at = 0
        for r0, h in rows:
            dst[r0 : r0 + h, SAMP : SAMP + 128] = tail[at : at + h]
            at += h

    inner, edges, alone = ((16, 96),), ((0, 16), (112, 16)), ((0, 32),)

    def inner_pass(s):
        cpi[:, 128 : SAMP + 128] = jnp.dot(
            b_in, xs[s, 16:144, :], preferred_element_type=f32
        ).astype(bf)
        prev = jnp.zeros((96, 64), bf)
        total = jnp.zeros((96, 256), f32)
        for b, results in time_blocks(cpi, wm[...], 0, 32, 8):
            for r in results:
                total = total + r * r
            prev = store_w(wt.at[s], ROWS, inner, b, results, prev)
        finish_w(wt.at[s], inner, prev)
        acc[s, 16:112, :] = total

    def edge_chan(s, lo, hi):
        both = jnp.concatenate([xs[s, 0:48, lo:hi], xs[s, 112:160, lo:hi]], axis=0)
        cpe[:, 128 + lo : 128 + hi] = jnp.dot(b_ed, both, preferred_element_type=f32).astype(bf)

    def edge_time(s, b0, b1, state):
        prev, total = state
        dst, half, rows = (wte, 32, alone) if s == 2 else (wt.at[s], ROWS, edges)
        for b, results in time_blocks(cpe, wm[...], b0, b1, 16):
            for r in results:
                total = total + r * r
            prev = store_w(dst, half, rows, b, results, prev)
        if b1 == 32:
            finish_w(dst, rows, prev)
            if s == 2:
                eacc[...] = total
            else:
                acc[s, 0:16, :] = total[0:16]
                acc[s, 112:128, :] = total[16:32]
        return prev, total

    def edge_state():
        return jnp.zeros((32, 64), bf), jnp.zeros((32, 256), f32)

    def panel(s):
        x0 = pag[s, 0].astype(f32)[:, 0:128]
        x7 = pag[s, 7].astype(f32)[:, 128:256]
        z4 = jnp.zeros((4, 128), f32)
        pcp[:, 0:128] = jnp.concatenate([z4, x7[0:12]], axis=0).astype(bf)
        pcp[:, QUART + 128 : QUART + 256] = jnp.concatenate([x0[4:16], z4], axis=0).astype(bf)
        for g in range(8):
            pcp[:, 128 + 256 * g : 384 + 256 * g] = pag[s, g]
        (_, res), = time_blocks(pcp, wm[...], 0, 8, 8)
        tot = res[0] * res[0]
        for r in res[1:]:
            tot = tot + r * r
        tot = jnp.sum(tot, axis=1, keepdims=True)
        tot = tot[0:4] + tot[4:8] + tot[8:12] + tot[12:16]
        scale = lax.rsqrt(tot * (1.0 / SAMP) + 1e-6)
        scale = jnp.concatenate([scale] * 4, axis=0)
        full = jnp.concatenate([(r * scale).astype(bf).astype(f32) for r in res], axis=1)
        for q in range(4):
            pwn[s, 0:4, 128 + QUART * q : 128 + QUART * (q + 1)] = full[4 * q : 4 * q + 4]

    def build_piece(s, lo, hi):
        dst = pm2 if s == 2 else pm
        for k in range(SRC):
            row = pwn[s, k : k + 1, lo : hi + 128]
            dst[64 * k : 64 * k + 64, lo:hi] = skewed(row, 64, 0)[:, 128:].astype(bf)
        late = pwn[s, :, lo + 64 : hi + 64]
        dst[256:272, lo:hi] = jnp.concatenate([late, late], axis=0).astype(bf)

    def build_p(s):
        for lo in range(0, SAMP + 128, 2048):
            build_piece(s, lo, min(lo + 2048, SAMP + 128))

    def matmul_nt(lhs, rhs):
        return lax.dot_general(lhs, rhs, (((1,), (1,)), ((), ())), preferred_element_type=f32)

    def corr(s):
        hi = SAMP + 128
        rr[...] = matmul_nt((pm2 if s == 2 else pm)[:, 0:hi], wt[s, :, 0:hi])

    def edge_corr(lo, hi, first):
        d = matmul_nt(pm2[:, lo:hi], wte[:, lo:hi])
        re[...] = d if first else re[...] + d

    def scales(sums):
        power = jnp.sum(jnp.transpose(sums), axis=0, keepdims=True)
        scale = lax.rsqrt(power * (1.0 / SAMP) + 1e-6)
        return jnp.concatenate([scale, scale], axis=1)

    def z_peer(i):
        return (c, (w // 4) * 4 + lax.rem(w + i, 4))

    z_me = lax.rem(w, 4)

    def z_copy(s, i):
        dev = z_peer(i)
        return remote(
            zsrc.at[s, lax.rem(w + i, 4)], zland.at[s, i], zs.at[4 * s + i], zr.at[4 * s + i], dev
        )

    def v_copy(s):
        return remote(vsrc.at[s], vland.at[s], vs.at[s], vr.at[s], (c, lax.rem(w + 4, 8)))

    def a_copy(s, i):
        return remote(red.at[s], agl.at[s, z_me], as_.at[4 * s + i], ar.at[4 * s + i], z_peer(i))

    def e_copy(i):
        return remote(esrc, eland.at[w], es.at[i], er.at[i], win_peer(c, w, i))

    norm = 1.0 / 256.0

    def send_corr(s):
        val = rr[...] * scales(acc[s])
        lates[s] = val[256:264, 128:256]
        val = val.astype(bf)
        for k in range(SRC):
            zsrc[s, k, 0:64] = val[64 * k : 64 * k + 64]
        for i in range(1, 4):
            z_copy(s, i).start()

    def sum_z(s):
        for i in range(1, 4):
            z_copy(s, i).wait()
        tot = zsrc[s, z_me].astype(f32)
        for i in range(1, 4):
            tot = tot + zland[s, i].astype(f32)
        vsrc[s] = tot.astype(bf)
        v_copy(s).start()

    def sum_y(s):
        v_copy(s).wait()
        val = ((vsrc[s].astype(f32) + vland[s].astype(f32)) * norm).astype(bf)
        red[s] = val
        for i in range(1, 4):
            a_copy(s, i).start()
        agl[s, z_me] = val

    def wait_all(s):
        for i in range(1, 4):
            a_copy(s, i).wait()

    def write_out(s):
        wait_all(s)
        for k in range(SRC):
            out[s, k, 0:64, :] = agl[s, k, :, 0:128]
            out[s, k, 64:128, :] = agl[s, k, :, 128:256]

    def send_edges():
        val = re[...] * scales(eacc[...])
        fold = jnp.concatenate([val[0:128], val[128:256]], axis=1)
        late = jnp.concatenate([val[256:260], val[256:260]], axis=1)
        late = jnp.concatenate([late] + [lates[s][0:4] for s in range(STEPS)], axis=0)
        val = jnp.concatenate([fold, late], axis=0).astype(bf)
        esrc[...] = val
        for i in range(1, 8):
            e_copy(i).start()
        eland[w] = val

    def add_edges():
        for i in range(1, 8):
            e_copy(i).wait()
        tot = eland[0].astype(f32)
        for i in range(1, 8):
            tot = tot + eland[i].astype(f32)
        tot = tot * norm

        def spread(rows, at):
            mid = jnp.zeros((rows.shape[0], 96), f32)
            return jnp.concatenate([rows[:, at : at + 16], mid, rows[:, at + 16 : at + 32]], axis=1)

        blank = jnp.zeros((15, ROWS), f32)
        for k in range(SRC):
            rows = tot[64 * (k % 2) : 64 * (k % 2) + 64]
            at = 64 * (k // 2)
            for a in range(2):
                val = agl[2, k, :, 128 * a : 128 * a + 128].astype(f32) + spread(rows, at + 32 * a)
                out[2, k, 64 * a : 64 * a + 64, :] = val.astype(bf)
            for s in range(STEPS):
                val = tot[132 + 4 * s + k : 133 + 4 * s + k]
                if s == 2:
                    val = val + spread(tot[128 + k : 129 + k], 32)
                out[s, k, 128:144, :] = jnp.concatenate([val, blank], axis=0).astype(bf)

    def reduce_panel(s):
        for i in range(1, 8):
            p_copy(s, i).wait()
        tot = part[s, g_me]
        for i in range(1, 8):
            tot = tot + pland[s, i]
        ysrc[s] = tot
        y_copy(s).start()

    def share_panel(s):
        y_copy(s).wait()
        val = (ysrc[s] + yland[s]).astype(bf)
        pbf[s] = val
        for i in range(1, 8):
            g_copy(s, i).start()
        pag[s, g_me] = val

    def wait_panel(s):
        for i in range(1, 8):
            g_copy(s, i).wait()

    def wait_halo(j):
        for cp in halos[j]:
            cp.wait()

    inner_pass(2)
    for s in ORDER:
        reduce_panel(s)
    for pair in halos[EARLY:]:
        for cp in pair:
            cp.start()
    inner_pass(0)
    inner_pass(1)
    for s in ORDER:
        share_panel(s)
    wait_halo(0)
    wait_halo(1)
    edge_chan(0, 0, SAMP)
    edge_time(0, 0, 32, edge_state())
    wait_panel(2)
    panel(2)
    build_p(2)
    corr(2)
    send_corr(2)
    wait_panel(0)
    panel(0)
    build_p(0)
    corr(0)
    send_corr(0)
    wait_panel(1)
    panel(1)
    build_p(1)
    sum_z(2)
    wait_halo(2)
    wait_halo(3)
    edge_chan(1, 0, SAMP)
    edge_time(1, 0, 32, edge_state())
    corr(1)
    send_corr(1)
    sum_z(0)
    wait_halo(4)
    edge_chan(2, 0, SAMP // 2)
    state = edge_time(2, 0, 15, edge_state())
    edge_corr(0, 3840, True)
    sum_z(1)
    sum_y(2)
    wait_halo(5)
    edge_chan(2, SAMP // 2, SAMP)
    edge_time(2, 15, 32, state)
    edge_corr(3840, SAMP + 128, False)
    send_edges()
    sum_y(0)
    sum_y(1)
    write_out(0)
    write_out(1)
    wait_all(2)
    add_edges()


def body(record, chan_taps, time_taps, sources):
    vm, dma = pltpu.VMEM, pltpu.SemaphoreType.DMA
    sm = pltpu.SMEM
    packed = pl.pallas_call(
        kernel,
        out_shape=jax.ShapeDtypeStruct((STEPS, SRC, 144, ROWS), bf),
        in_specs=[pl.BlockSpec(memory_space=pl.ANY)] * 4,
        out_specs=pl.BlockSpec(memory_space=pltpu.VMEM),
        scratch_shapes=[
            sm((CT,), f32),
            sm((TT,), f32),
            sm((STEPS, SRC), jnp.int32),
            dma((3,)),
            vm((STEPS, 160, SAMP), bf),
            vm((96, EXT), bf),
            vm((32, EXT), bf),
            vm((STEPS, 256, EXT), bf),
            vm((272, EXT), bf),
            vm((272, 256), f32),
            vm((STEPS, ROWS, 256), f32),
            vm((512, 256), bf),
            vm((STEPS, 8, 16, 256), f32),
            vm((STEPS, 8, 16, 256), f32),
            vm((STEPS, 16, 256), f32),
            vm((STEPS, 16, 256), f32),
            vm((STEPS, 16, 256), bf),
            vm((STEPS, 8, 16, 256), bf),
            vm((16, QUART + 256), bf),
            vm((STEPS, 8, EXT), f32),
            vm((STEPS, 4, 64, 256), bf),
            vm((STEPS, 4, 64, 256), bf),
            vm((STEPS, 64, 256), bf),
            vm((STEPS, 64, 256), bf),
            vm((STEPS, 64, 256), bf),
            vm((STEPS, 4, 64, 256), bf),
            vm((STEPS, 8, 128), f32),
            vm((64, EXT), bf),
            vm((272, EXT), bf),
            vm((272, 64), f32),
            vm((32, 256), f32),
            vm((144, 128), bf),
            vm((8, 144, 128), bf),
            dma((STEPS,)),
            dma((12,)), dma((12,)),
            dma((24,)), dma((24,)),
            dma((STEPS,)), dma((STEPS,)),
            dma((24,)), dma((24,)),
            dma((12,)), dma((12,)),
            dma((STEPS,)), dma((STEPS,)),
            dma((12,)), dma((12,)),
            dma((8,)), dma((8,)),
        ],
        compiler_params=pltpu.CompilerParams(
            collective_id=0, has_side_effects=True, vmem_limit_bytes=58 * 2**20
        ),
        name="xcorr",
    )(record, chan_taps, time_taps, sources)
    return packed[:, :, :129].astype(f32)


def solution(mesh):
    in_specs = (P(None, "chan", "win"), P(), P(), P())
    out_specs = P(None, None, None, "chan")
    return jax.shard_map(body, mesh=mesh, in_specs=in_specs, out_specs=out_specs, check_vma=False)
```
